256 devices in a mesh: lon: 32 (over x_lo, z, core), lat: 8 (over x_hi, y).
Axes of the slice: x: 4 (x_hi: 2, x_lo: 2; x = x_hi * 2 + x_lo), y: 4, z: 8, core: 2. Of those that a mesh axis runs over, the one named last changes fastest.
Arguments:
- pixels: float32 [32, 32, 4096], P('lon', 'lat'), may hold values from -6 to 6
- patch_w: bfloat16 [32, 4, 1024], P('lon'), may hold values from -3 to 3
- var_embed: bfloat16 [32, 1024], replicated, may hold values from -6 to 6
- var_ids: int32 [32], replicated, may hold values from 0 to 31, each once
- agg_score: bfloat16 [1024, 16], replicated
- agg_value: bfloat16 [1024, 1024], replicated, may hold values from -0.1875 to 0.1875
- agg_out: bfloat16 [1024, 1024], replicated, may hold values from -0.1875 to 0.1875
- pos_embed: bfloat16 [16, 2048, 1024], P('lat', 'lon'), may hold values from -3 to 3
- norm_gain: float32 [1024], replicated, may hold values from 0.5 to 1.5
- w_query: bfloat16 [1024, 1024], replicated
- w_key: bfloat16 [1024, 1024], replicated
- w_value: bfloat16 [1024, 1024], replicated, may hold values from -0.1875 to 0.1875
- w_proj: bfloat16 [1024, 1024], replicated, may hold values from -0.1875 to 0.1875
- window_off: int32 [16], replicated, may hold values from -32 to 32
Outputs:
- updated: bfloat16 [16, 2048, 1024], P('lat', 'lon')
The draws below stay inside these ranges and needn't reach their ends.
Inputs may be any that keep to these rules, and one draw needn't show every extreme that they name: `var_ids`: each variable number appears once.
All inputs are finite; a program needn't handle non-finite values.
Results may differ from the reference program's by a relative error of at most 0.015.
The reference program's roundings to bfloat16 on the way count: a program that leaves them out, or rounds other values in their place, can miss the bound.
Values may be sent and summed in bfloat16 or wider, within the bound.
A program may use at most 128 MiB of HBM per device.

```python
import math
import jax
import jax.numpy as jnp
from jax import lax

D = 1024
HEADS = 16
HEAD_DIM = 64
COL_DEV = 64
VARS = 32
ROWS = 16
COLS = 2048
RADIUS = 16
OFF_MAX = 32


def shared_base(key):
    return jnp.clip(jax.random.normal(key, (D, D), jnp.float32), -6.0, 6.0)


def draw_w_key(key, part):
    common = shared_base(key)
    return (common / math.sqrt(D)).astype(jnp.bfloat16)


def draw_w_query(key, part):
    key = jax.random.fold_in(key, 12)
    own_part = jnp.clip(jax.random.normal(key, (D, D), jnp.float32), -6.0, 6.0)
    return (own_part / math.sqrt(D)).astype(jnp.bfloat16)


def draw_agg_score(key, part):
    key = jax.random.fold_in(key, 13)
    values = jnp.clip(jax.random.normal(key, (D, HEADS), jnp.float32), -6.0, 6.0)
    return (values * (1.5 / math.sqrt(D))).astype(jnp.bfloat16)


def plant(values, rng, smallest, largest):
    spot = [jax.random.randint(jax.random.fold_in(rng, axis), (), 0, length) for axis, length in enumerate(values.shape)]
    main_axis = values.shape.index(max(values.shape))
    next_to = spot[:main_axis] + [(spot[main_axis] + 1) % values.shape[main_axis]] + spot[main_axis + 1:]
    return values.at[tuple(spot)].set(smallest).at[tuple(next_to)].set(largest)


def steps_of(rng, extent, split, least, high):
    level = 1.0
    for position, parts in split:
        draws = jax.random.uniform(jax.random.fold_in(jax.random.fold_in(rng, 6), position), (parts,), jnp.float32, least / len(split), high / len(split))
        level = level * jnp.repeat(jnp.exp(draws), extent[position] // parts).reshape((-1,) + (1,) * (len(extent) - 1 - position))
    return level


def gaussian(own_key, shape, scale, limit, split=(), kind=jnp.bfloat16):
    drawn = scale * jax.random.normal(own_key, shape, jnp.float32)
    if split:
        drawn = drawn * steps_of(own_key, shape, split, -0.22, 0.18)
    return jnp.clip(drawn, -limit, limit).astype(kind)


def setup_inputs(seed: int = 0) -> dict:
    keys = jax.random.split(jax.random.key(seed), 15)
    pixels = gaussian(keys[0], (VARS, 2 * ROWS, 2 * COLS), 1.0, 6.0, ((0, 32), (1, 8)), jnp.float32)
    patch_w = gaussian(keys[1], (VARS, 4, D), 4 ** -0.5, 3.0, ((0, 32),))
    var_embed = gaussian(keys[2], (VARS, D), 1.0, 6.0)
    var_ids = jax.random.permutation(keys[3], VARS).astype(jnp.int32)
    agg_score = draw_agg_score(jax.random.fold_in(keys[14], 71), 0)
    agg_value = gaussian(keys[5], (D, D), D ** -0.5, 0.1875)
    agg_out = gaussian(keys[6], (D, D), D ** -0.5, 0.1875)
    pos_embed = gaussian(keys[7], (ROWS, COLS, D), 0.5, 3.0, ((0, 8), (1, 32)))
    norm_gain = jnp.clip(1.0 + 0.1 * jax.random.normal(keys[8], (D,), jnp.float32), 0.5, 1.5)
    w_query = draw_w_query(jax.random.fold_in(keys[14], 71), 0)
    w_key = draw_w_key(jax.random.fold_in(keys[14], 71), 0)
    w_value = gaussian(keys[11], (D, D), D ** -0.5, 0.1875)
    w_proj = gaussian(keys[12], (D, D), D ** -0.5, 0.1875)
    window_off = plant(jax.random.randint(keys[13], (HEADS,), 0 - OFF_MAX, OFF_MAX + 1), jax.random.fold_in(keys[13], 1), 0 - OFF_MAX, OFF_MAX).astype(jnp.int32)
    return {"pixels": pixels, "patch_w": patch_w, "var_embed": var_embed, "var_ids": var_ids, "agg_score": agg_score, "agg_value": agg_value, "agg_out": agg_out, "pos_embed": pos_embed, "norm_gain": norm_gain, "w_query": w_query, "w_key": w_key, "w_value": w_value, "w_proj": w_proj, "window_off": window_off}


def variable_vectors(var_ids, var_embed):
    count = var_embed.shape[0]
    onehot = (var_ids[:, None] == jnp.arange(count, dtype=jnp.int32)[None, :]).astype(jnp.float32)
    return jnp.dot(onehot, var_embed.astype(jnp.float32), precision=lax.Precision.HIGHEST)

def embed_patches(pixel_block, patch_w, vectors):
    nvar, two_rows, two_cols = pixel_block.shape
    patches = pixel_block.reshape(nvar, two_rows // 2, 2, two_cols // 2, 2)
    patches = patches.transpose(0, 1, 3, 2, 4).reshape(nvar, two_rows // 2, two_cols // 2, 4)
    result = jnp.einsum('vrck,vkd->vrcd', patches, patch_w.astype(jnp.float32), precision=lax.Precision.HIGHEST)
    return (result + vectors[:, None, None, :]).astype(jnp.bfloat16)

def aggregate(embedded, agg_score, agg_value, agg_out):
    nvar, row_count, col_count, width = embedded.shape
    flat = embedded.reshape(nvar, row_count * col_count, width).astype(jnp.float32)
    scores = jnp.einsum('vtd,dh->vth', flat, agg_score.astype(jnp.float32))
    weights = jax.nn.softmax(scores, axis=0).astype(jnp.bfloat16)
    mixture = jnp.einsum('vth,vtd->thd', weights.astype(jnp.float32), flat).astype(jnp.bfloat16)
    value_heads = agg_value.reshape(width, HEADS, HEAD_DIM).astype(jnp.float32)
    head_out = jnp.einsum('thd,dhe->the', mixture.astype(jnp.float32), value_heads).astype(jnp.bfloat16)
    head_out = head_out.reshape(row_count * col_count, width)
    return jnp.dot(head_out, agg_out, preferred_element_type=jnp.float32).reshape(row_count, col_count, width)

def layer_norm(tokens, norm_gain):
    center = tokens - lax.optimization_barrier(jnp.mean(tokens, axis=-1, keepdims=True))
    spread = lax.optimization_barrier(jnp.mean(center * center, axis=-1, keepdims=True))
    return (center * lax.rsqrt(spread + 1e-05) * norm_gain).astype(jnp.bfloat16)

def attend(queries, key_block, value_block, window_off, col_dev):
    width = queries.shape[-1]
    query_heads = queries.reshape(-1, HEADS, HEAD_DIM).astype(jnp.float32)
    key_heads = key_block.reshape(-1, HEADS, HEAD_DIM).astype(jnp.float32)
    value_heads = value_block.reshape(-1, HEADS, HEAD_DIM).astype(jnp.float32)
    logits = jnp.einsum('qhe,khe->hqk', query_heads, key_heads) / jnp.sqrt(jnp.float32(HEAD_DIM))
    query_col = jnp.arange(query_heads.shape[0], dtype=jnp.int32) % col_dev
    key_col = jnp.arange(key_heads.shape[0], dtype=jnp.int32) % (3 * col_dev)
    col_gap = key_col[None, :] - col_dev - query_col[:, None]
    allowed = jnp.abs(col_gap[None, :, :] - window_off[:, None, None]) <= RADIUS
    logits = jnp.where(allowed, logits, jnp.float32(-1e+30))
    weights = jax.nn.softmax(logits, axis=-1).astype(jnp.bfloat16)
    result = jnp.einsum('hqk,khe->qhe', weights.astype(jnp.float32), value_heads)
    return result.astype(jnp.bfloat16).reshape(-1, width)

def reference(pixels, patch_w, var_embed, var_ids, agg_score, agg_value, agg_out, pos_embed, norm_gain, w_query, w_key, w_value, w_proj, window_off):
    blocks = COLS // COL_DEV
    vectors = variable_vectors(var_ids, var_embed)

    def token_block(block):
        pixel_block = lax.dynamic_slice_in_dim(pixels, block * 2 * COL_DEV, 2 * COL_DEV, 2)
        embedded = embed_patches(pixel_block, patch_w, vectors)
        return aggregate(embedded, agg_score, agg_value, agg_out)
    mixed_tokens = lax.map(token_block, jnp.arange(blocks, dtype=jnp.int32))
    tokens = mixed_tokens.transpose(1, 0, 2, 3).reshape(ROWS, COLS, D) + pos_embed.astype(jnp.float32)
    normed = layer_norm(tokens, norm_gain).reshape(ROWS * COLS, D)
    query_all = jnp.dot(normed, w_query, preferred_element_type=jnp.float32).astype(jnp.bfloat16).reshape(ROWS, COLS, D)
    key_all = jnp.dot(normed, w_key, preferred_element_type=jnp.float32).astype(jnp.bfloat16).reshape(ROWS, COLS, D)
    value_all = jnp.dot(normed, w_value, preferred_element_type=jnp.float32).astype(jnp.bfloat16).reshape(ROWS, COLS, D)

    def attend_block(block):
        query_block = lax.dynamic_slice_in_dim(query_all, block * COL_DEV, COL_DEV, 1).reshape(-1, D)
        columns = (block * COL_DEV - COL_DEV + jnp.arange(3 * COL_DEV, dtype=jnp.int32)) % COLS
        key_block = jnp.take(key_all, columns, axis=1).reshape(-1, D)
        value_block = jnp.take(value_all, columns, axis=1).reshape(-1, D)
        attended = attend(query_block, key_block, value_block, window_off, COL_DEV)
        token_part = lax.dynamic_slice_in_dim(tokens, block * COL_DEV, COL_DEV, 1).reshape(-1, D)
        result = token_part + jnp.dot(attended, w_proj, preferred_element_type=jnp.float32)
        return result.astype(jnp.bfloat16).reshape(ROWS, COL_DEV, D)
    outcome = lax.map(attend_block, jnp.arange(blocks, dtype=jnp.int32))
    return outcome.transpose(1, 0, 2, 3).reshape(ROWS, COLS, D)
```

```python
import jax
import jax.numpy as jnp
from jax import lax
from jax.sharding import PartitionSpec as P

HEADS = 16
HEAD_DIM = 64
RADIUS = 16
OFF_MAX = 32


def from_behind(block, axis, distance):
    devices = range(lax.axis_size(axis))
    route = [((i - distance) % len(devices), i) for i in devices]
    return lax.ppermute(block, axis, route)


def variable_vectors(var_ids, var_embed):
    count = var_embed.shape[0]
    onehot = (var_ids[:, None] == jnp.arange(count, dtype=jnp.int32)[None, :]).astype(jnp.float32)
    return jnp.dot(onehot, var_embed.astype(jnp.float32), precision=lax.Precision.HIGHEST)


def embed_patches(pixel_block, patch_w, vectors):
    nvar, two_rows, two_cols = pixel_block.shape
    patches = pixel_block.reshape(nvar, two_rows // 2, 2, two_cols // 2, 2)
    patches = patches.transpose(0, 1, 3, 2, 4).reshape(nvar, two_rows // 2, two_cols // 2, 4)
    result = jnp.einsum(
        "vrck,vkd->vrcd", patches, patch_w.astype(jnp.float32), precision=lax.Precision.HIGHEST
    )
    return (result + vectors[:, None, None, :]).astype(jnp.bfloat16)


def aggregate(embedded, agg_score, agg_value, agg_out):
    nvar, row_count, col_count, width = embedded.shape
    flat = embedded.reshape(nvar, row_count * col_count, width)
    scores = jnp.einsum("vtd,dh->vth", flat, agg_score, preferred_element_type=jnp.float32)
    weights = jax.nn.softmax(scores, axis=0).astype(jnp.bfloat16)
    mixture = jnp.einsum("vth,vtd->thd", weights, flat, preferred_element_type=jnp.float32).astype(
        jnp.bfloat16
    )
    value_heads = agg_value.reshape(width, HEADS, HEAD_DIM)
    head_out = jnp.einsum(
        "thd,dhe->the", mixture, value_heads, preferred_element_type=jnp.float32
    ).astype(jnp.bfloat16)
    head_out = head_out.reshape(row_count * col_count, width)
    return jnp.dot(head_out, agg_out, preferred_element_type=jnp.float32).reshape(
        row_count, col_count, width
    )


def layer_norm(tokens, norm_gain):
    center = tokens - jnp.mean(tokens, axis=-1, keepdims=True)
    spread = jnp.mean(center * center, axis=-1, keepdims=True)
    return (center * lax.rsqrt(spread + 1e-05) * norm_gain).astype(jnp.bfloat16)


def attend(query_heads, key_heads, value_heads):
    row_count, col_count, width = query_heads.shape
    logits = jnp.einsum("rce,sde->rcsd", query_heads, key_heads, preferred_element_type=jnp.float32)
    logits = logits / jnp.sqrt(jnp.float32(HEAD_DIM))
    gap = jnp.arange(key_heads.shape[1])[None, :] - jnp.arange(col_count)[:, None]
    allowed = (gap >= 0) & (gap <= 2 * RADIUS)
    logits = jnp.where(allowed[None, :, None, :], logits, jnp.float32(-1e30))
    weights = jax.nn.softmax(logits, axis=(-2, -1)).astype(jnp.bfloat16)
    result = jnp.einsum("rcsd,sde->rce", weights, value_heads, preferred_element_type=jnp.float32)
    return result.astype(jnp.bfloat16)


def per_device(
    pixels,
    patch_w,
    var_embed,
    var_ids,
    agg_score,
    agg_value,
    agg_out,
    pos_embed,
    norm_gain,
    w_query,
    w_key,
    w_value,
    w_proj,
    window_off,
):
    vectors = variable_vectors(var_ids, var_embed)
    all_pixels = lax.all_to_all(pixels, "lon", split_axis=2, concat_axis=0, tiled=True)
    all_weights = lax.all_gather(patch_w, "lon", axis=0, tiled=True)
    embedded = embed_patches(all_pixels, all_weights, vectors)
    mixed_tokens = aggregate(embedded, agg_score, agg_value, agg_out)
    row_count, col_count, width = pos_embed.shape
    tokens = mixed_tokens + pos_embed.astype(jnp.float32)
    normed = layer_norm(tokens, norm_gain).reshape(row_count * col_count, width)
    queries = jnp.dot(normed, w_query, preferred_element_type=jnp.float32).astype(jnp.bfloat16)
    key_rows = jnp.dot(normed, w_key, preferred_element_type=jnp.float32).astype(jnp.bfloat16)
    value_rows = jnp.dot(normed, w_value, preferred_element_type=jnp.float32).astype(jnp.bfloat16)
    lat_count = lax.axis_size("lat")
    lat_index = lax.axis_index("lat")
    share = width // lat_count
    heads_dev = share // HEAD_DIM
    halo = OFF_MAX + RADIUS
    packed = jnp.stack([queries, key_rows, value_rows]).reshape(3, row_count, col_count, width)
    packed = lax.all_to_all(packed, "lat", split_axis=3, concat_axis=1, tiled=True)
    key_value = packed[1:]
    western = from_behind(key_value[:, :, col_count - halo :], "lon", 1)
    eastern = from_behind(key_value[:, :, :halo], "lon", -1)
    window_set = jnp.concatenate([western, key_value, eastern], axis=2)
    parts = []
    for head in range(heads_dev):
        off = lax.dynamic_index_in_dim(window_off, lat_index * heads_dev + head, 0, False)
        part = slice(head * HEAD_DIM, (head + 1) * HEAD_DIM)
        own = lax.dynamic_slice_in_dim(
            window_set[..., part], off + OFF_MAX, col_count + 2 * RADIUS, 2
        )
        parts.append(attend(packed[0, :, :, part], own[0], own[1]))
    attended = jnp.concatenate(parts, axis=-1)
    attended = lax.all_to_all(attended, "lat", split_axis=0, concat_axis=2, tiled=True)
    attended = attended.reshape(-1, width)
    result = tokens.reshape(row_count * col_count, width) + jnp.dot(
        attended, w_proj, preferred_element_type=jnp.float32
    )
    return result.astype(jnp.bfloat16).reshape(row_count, col_count, width)


def solution(mesh):
    placed = (
        P("lon", "lat", None),
        P("lon", None, None),
        P(),
        P(),
        P(),
        P(),
        P(),
        P("lat", "lon", None),
        P(),
        P(),
        P(),
        P(),
        P(),
        P(),
    )
    return jax.shard_map(
        per_device, mesh=mesh, in_specs=placed, out_specs=P("lat", "lon", None), check_vma=False
    )
```

```python
import functools
import jax
import jax.numpy as jnp
from jax import lax
from jax.experimental import pallas as pl
from jax.experimental.pallas import tpu as pltpu
from jax.sharding import PartitionSpec as P

HEADS = 16
HEAD_DIM = 64
RADIUS = 16
OFF_MAX = 32
HALO = RADIUS + OFF_MAX
VARS = 32
WIDTH = 1024
COLS = 64
FRAME = COLS + 2 * HALO
LON = 32
LAT = 8
LANES = 128
GROUP = 16
SPAN = 64
SHIFTED = COLS - GROUP + SPAN
MASKED = -1e30
F32 = jnp.float32
BF16 = jnp.bfloat16
MESH = pl.DeviceIdType.MESH


def iota(shape, dim):
    return lax.broadcasted_iota(jnp.int32, shape, dim)


def dot(a, b):
    return jnp.dot(a, b, preferred_element_type=F32)


def dot_nt(a, b):
    return lax.dot_general(a, b, (((1,), (1,)), ((), ())), preferred_element_type=F32)


def dot_tn(a, b):
    return lax.dot_general(a, b, (((0,), (0,)), ((), ())), preferred_element_type=F32)


def roll(x, shift):
    return pltpu.roll(x, shift, 1)


def make_constants(sel, vmask, tmask):
    source = iota((256, 256), 0)
    target = (
        (source % 4) // 2 * LANES
        + (source % LANES) // 4 * 4
        + source % 2 * 2
        + source // LANES
    )
    sel[...] = (iota((256, 256), 1) == target).astype(F32).astype(BF16)
    lane = iota((256, 256), 1)
    slot = iota((256, 256), 0) // GROUP
    mine = jnp.where(lane < 192, (lane % 64) // 4, jnp.where(lane < 208, lane - 192, -1))
    vmask[...] = (mine == slot).astype(F32).astype(BF16)
    tmask[...] = (iota((GROUP, 512), 1) % GROUP == iota((GROUP, 512), 0)).astype(F32)


def variable_rows(ids, var_embed, vectors):
    onehot = (iota((VARS, VARS), 0) == ids[...]).astype(F32).astype(BF16)
    vectors[...] = dot_tn(onehot, var_embed[...]).astype(BF16)


def embedding_weights(pw_all, vectors, wflat, wk):
    for v in range(VARS):
        wflat[4 * v : 4 * v + 4, :] = pw_all[v].astype(F32)
    for half in range(2):
        part = wflat[64 * half : 64 * half + 64, :].astype(BF16)
        for piece in range(3):
            wk[half, 64 * piece : 64 * piece + 64, :] = part
        wk[half, 192:208, :] = vectors[16 * half : 16 * half + 16, :]
        wk[half, 208:256, :] = jnp.zeros((48, WIDTH), BF16)


def patch_rows(pix_all, flat, turned, sel, base):
    for v in range(VARS):
        flat[4 * v : 4 * v + 4, :] = pix_all[v]
    turned[...] = flat[...].T
    points = jnp.concatenate(
        [turned[pl.ds(0, COLS, stride=2), :], turned[pl.ds(1, COLS, stride=2), :]], axis=1
    )
    pieces = []
    rest = points
    for _ in range(3):
        part = rest.astype(BF16)
        rest = rest - part.astype(F32)
        pieces.append(dot(part, sel[...]))
    lane = iota((COLS, LANES), 1)
    low = lane < 64
    ones = ((lane >= 64) & (lane < 80)).astype(F32)
    for r in range(2):
        hi, mid, lo = (piece[:, r * LANES : (r + 1) * LANES] for piece in pieces)
        base[r, 0, :, :LANES] = jnp.where(low, hi, roll(mid, 64)).astype(BF16)
        base[r, 0, :, LANES:] = jnp.where(low, lo, ones).astype(BF16)
        base[r, 1, :, :LANES] = jnp.where(low, roll(hi, 64), mid).astype(BF16)
        base[r, 1, :, LANES:] = jnp.where(low, roll(lo, 64), ones).astype(BF16)


def over_variables(x, op):
    parts = [x[:, LANES * i : LANES * (i + 1)] for i in range(4)]
    total = op(op(parts[0], parts[1]), op(parts[2], parts[3]))
    for shift in (16, 32, 64):
        total = op(total, roll(total, shift))
    return jnp.concatenate([total] * 4, axis=1)


def aggregate_group(r, g, base, vmask, tmask, wk, score_t, embedded, mixture):
    rows = pl.ds(pl.multiple_of(g * GROUP, GROUP), GROUP)
    for half in range(2):
        points = base[r, half, rows, :]
        spread = jnp.concatenate([points] * 16, axis=0) * vmask[...]
        embedded[256 * half : 256 * half + 256, :] = dot(spread, wk[half]).astype(BF16)
    scores = dot_nt(score_t[...], embedded[...])
    power = jnp.exp(scores - over_variables(scores, jnp.maximum))
    weights = (power / over_variables(power, jnp.add)).astype(BF16).astype(F32)
    blocks = [
        jnp.broadcast_to(weights[h : h + 1, :], (GROUP, 512)) * tmask[...] for h in range(HEADS)
    ]
    blocks = jnp.concatenate(blocks, axis=0).astype(BF16)
    mixed = dot(blocks, embedded[...]).astype(BF16)
    mixture[:, rows, :] = mixed.reshape(HEADS, GROUP, WIDTH)


def head_outputs(mixture, agg_value, head_out):
    low = iota((COLS, LANES), 1) < 64
    for quad in range(4):
        rows = mixture[4 * quad : 4 * quad + 4].reshape(4 * COLS, WIDTH)
        out = dot(rows, agg_value[:, 256 * quad : 256 * quad + 256])
        for pair in range(2):
            lanes = slice(LANES * pair, LANES * (pair + 1))
            first = out[2 * pair * COLS : (2 * pair + 1) * COLS, lanes]
            second = out[(2 * pair + 1) * COLS : (2 * pair + 2) * COLS, lanes]
            at = 256 * quad + LANES * pair
            head_out[:, at : at + LANES] = jnp.where(low, first, second).astype(BF16)


def layer_norm(tokens, norm_gain):
    center = tokens - jnp.mean(tokens, axis=-1, keepdims=True)
    spread = jnp.mean(center * center, axis=-1, keepdims=True)
    return (center * lax.rsqrt(spread + 1e-05) * norm_gain).astype(BF16)


def window_bias(head, residual):
    other = 64 * (1 - head)
    lane = iota((SPAN, LANES), 1) - other
    gap = iota((SPAN, LANES), 0) - lane - residual
    hidden = (lane >= 0) & (lane < GROUP) & ((gap < 0) | (gap > 2 * RADIUS))
    return jnp.where(hidden, F32(MASKED), F32(0)).astype(BF16)


def shift_windows(s, step, win, shifted):
    for r in range(2):
        for part in range(2):
            rows = jnp.zeros((SHIFTED, LANES), BF16)
            for i in range(5):
                count = min(SHIFTED, FRAME - GROUP * i)
                piece = win[r, part, s, GROUP * i : GROUP * i + count, :]
                if count < SHIFTED:
                    piece = jnp.concatenate(
                        [piece, jnp.zeros((SHIFTED - count, LANES), BF16)], axis=0
                    )
                rows = jnp.where(step == i, piece, rows)
            shifted[r, part, s] = rows


def attend_block(first, biases, query_win, shifted, attended):
    cols = pl.ds(pl.multiple_of(first, GROUP), GROUP)
    span = pl.ds(pl.multiple_of(first, GROUP), SPAN)
    lane_q = iota((GROUP, LANES), 1)
    row_q = iota((GROUP, LANES), 0)
    lane_k = iota((SPAN, LANES), 1)
    outs = []
    for head in range(2):
        own_q = (lane_q < 64) if head == 0 else (lane_q >= 64)
        own_k = (lane_k < 64) if head == 0 else (lane_k >= 64)
        pick = (lane_q - 64 * (1 - head) == row_q).astype(F32).astype(BF16)
        scale = BF16(0.125)
        rows = [(r, s) for r in range(2) for s in range(LAT)]
        queries = [jnp.where(own_q, query_win[r, s, cols, :] * scale, pick) for r, s in rows]
        keys = [jnp.where(own_k, shifted[r, 0, s, span, :], biases[head]) for r, s in rows]
        values = [shifted[r, 1, s, span, :] for r, s in rows]
        logits = dot_nt(jnp.concatenate(queries, axis=0), jnp.concatenate(keys, axis=0))
        power = jnp.exp(logits - jnp.max(logits, axis=1, keepdims=True))
        weights = power * (1.0 / jnp.sum(power, axis=1, keepdims=True))
        outs.append(dot(weights.astype(BF16), jnp.concatenate(values, axis=0)))
    low = iota((256, LANES), 1) < 64
    result = jnp.where(low, outs[0], outs[1]).astype(BF16)
    for r in range(2):
        for s in range(LAT):
            at = (r * LAT + s) * GROUP
            attended[s, r, cols, :] = result[at : at + GROUP, :]


def kernel(
    pixels,
    patch_w,
    var_embed,
    ids,
    agg_score,
    agg_value,
    agg_out,
    pos_embed,
    norm_gain,
    w_query,
    w_key,
    w_value,
    w_proj,
    window_off,
    updated,
    pix_all,
    pw_all,
    ve,
    score,
    score_t,
    value_w,
    out_w,
    pos,
    query_w,
    key_w,
    val_w,
    proj_w,
    sel,
    vmask,
    tmask,
    vectors,
    wflat,
    wk,
    flat,
    turned,
    base,
    embedded,
    mixture,
    head_out,
    tokens,
    normed,
    query_own,
    kv_own,
    query_win,
    win,
    shifted,
    attended,
    attended_own,
    load_sem,
    pix_sem,
    pw_sem,
    kv_sem,
    kv_send,
    q_sem,
    q_send,
    halo_sem,
    halo_send,
    att_sem,
    att_send,
):
    lon = lax.axis_index("lon")
    lat = lax.axis_index("lat")
    loads = [
        pltpu.make_async_copy(src, dst, load_sem.at[i])
        for i, (src, dst) in enumerate(
            (
                (var_embed, ve),
                (agg_score, score),
                (agg_value, value_w),
                (agg_out, out_w),
                (pos_embed, pos),
                (w_key, key_w),
                (w_value, val_w),
                (w_query, query_w),
                (w_proj, proj_w),
            )
        )
    ]
    barrier = pltpu.get_barrier_semaphore()

    @pl.loop(1, LON)
    def _(d):
        pl.semaphore_signal(
            barrier, inc=1, device_id={"lon": lax.rem(lon + d, LON)}, device_id_type=MESH
        )

    @pl.loop(1, LAT)
    def _(d):
        pl.semaphore_signal(
            barrier, inc=1, device_id={"lat": lax.rem(lat + d, LAT)}, device_id_type=MESH
        )

    def pixel_part(to):
        return pixels.at[0, :, pl.ds(pl.multiple_of(to * LANES, LANES), LANES)]

    own_pix = pltpu.make_async_copy(pixel_part(lon), pix_all.at[lon], pix_sem.at[0])
    own_pw = pltpu.make_async_copy(patch_w.at[0], pw_all.at[lon], pw_sem.at[0])
    own_pix.start()
    own_pw.start()
    for load in loads:
        load.start()
    make_constants(sel, vmask, tmask)
    pl.semaphore_wait(barrier, LON + LAT - 2)

    @pl.loop(1, LON)
    def _(d):
        to = lax.rem(lon + d, LON)
        pltpu.make_async_remote_copy(
            src_ref=pixel_part(to),
            dst_ref=pix_all.at[lon],
            send_sem=pix_sem.at[1],
            recv_sem=pix_sem.at[0],
            device_id={"lon": to},
            device_id_type=MESH,
        ).start()
        pltpu.make_async_remote_copy(
            src_ref=patch_w.at[0],
            dst_ref=pw_all.at[lon],
            send_sem=pw_sem.at[1],
            recv_sem=pw_sem.at[0],
            device_id={"lon": to},
            device_id_type=MESH,
        ).start()

    loads[0].wait()
    variable_rows(ids, ve, vectors)
    loads[1].wait()
    identity = (iota((HEADS, HEADS), 0) == iota((HEADS, HEADS), 1)).astype(F32).astype(BF16)
    score_t[...] = dot_nt(identity, score[...]).astype(BF16)

    def wait_bytes(ref, sem):
        pltpu.make_async_copy(ref, ref, sem).wait()

    wait_bytes(pix_all, pix_sem.at[0])
    patch_rows(pix_all, flat, turned, sel, base)
    wait_bytes(pw_all, pw_sem.at[0])
    embedding_weights(pw_all, vectors, wflat, wk)

    def lanes_of(device):
        return pl.ds(pl.multiple_of(device * LANES, LANES), LANES)

    def kv_part(r, to):
        return kv_own.at[r, :, :, lanes_of(to)]

    def kv_place(r, s):
        return win.at[r, :, s, pl.ds(HALO, COLS), :]

    def send_to_all(part, place, send_sem, recv_sem):
        own = pltpu.make_async_copy(part(lat), place(lat), recv_sem)
        own.start()

        @pl.loop(1, LAT)
        def _(d):
            to = lax.rem(lat + d, LAT)
            pltpu.make_async_remote_copy(
                src_ref=part(to),
                dst_ref=place(lat),
                send_sem=send_sem,
                recv_sem=recv_sem,
                device_id={"lat": to},
                device_id_type=MESH,
            ).start()

    east_of = lax.rem(lon + 1, LON)
    west_of = lax.rem(lon + LON - 1, LON)

    def send_halos(r):
        @pl.loop(0, LAT)
        def _(d):
            s = lax.rem(lat + LAT - d, LAT)
            wait_bytes(kv_place(r, s), kv_sem.at[r, s])
            pltpu.make_async_remote_copy(
                src_ref=win.at[r, :, s, pl.ds(HALO + COLS - HALO, HALO), :],
                dst_ref=win.at[r, :, s, pl.ds(0, HALO), :],
                send_sem=halo_send.at[r, 0],
                recv_sem=halo_sem.at[r, 0],
                device_id={"lon": east_of},
                device_id_type=MESH,
            ).start()
            pltpu.make_async_remote_copy(
                src_ref=win.at[r, :, s, pl.ds(HALO, HALO), :],
                dst_ref=win.at[r, :, s, pl.ds(HALO + COLS, HALO), :],
                send_sem=halo_send.at[r, 1],
                recv_sem=halo_sem.at[r, 1],
                device_id={"lon": west_of},
                device_id_type=MESH,
            ).start()

    for r in range(2):

        @pl.loop(0, COLS // GROUP)
        def _(g):
            aggregate_group(r, g, base, vmask, tmask, wk, score_t, embedded, mixture)

        if r == 0:
            loads[2].wait()
        head_outputs(mixture, value_w, head_out)
        if r == 0:
            loads[3].wait()
            loads[4].wait()
        tokens[r] = dot(head_out[...], out_w[...]) + pos[r].astype(F32)
        normed[...] = layer_norm(tokens[r], norm_gain[...])
        if r == 0:
            loads[5].wait()
            loads[6].wait()
        kv_own[r, 0] = dot(normed[...], key_w[...]).astype(BF16)
        kv_own[r, 1] = dot(normed[...], val_w[...]).astype(BF16)
        own = pltpu.make_async_copy(kv_part(r, lat), kv_place(r, lat), kv_sem.at[r, lat])
        own.start()

        @pl.loop(1, LAT)
        def _(d):
            to = lax.rem(lat + d, LAT)
            pltpu.make_async_remote_copy(
                src_ref=kv_part(r, to),
                dst_ref=kv_place(r, lat),
                send_sem=kv_send.at[r],
                recv_sem=kv_sem.at[r, lat],
                device_id={"lat": to},
                device_id_type=MESH,
            ).start()

        if r == 0:
            loads[7].wait()
        query_own[r] = dot(normed[...], query_w[...]).astype(BF16)
        send_to_all(
            lambda to: query_own.at[r, :, lanes_of(to)],
            lambda s: query_win.at[r, s],
            q_send.at[r],
            q_sem.at[r],
        )
        if r == 1:
            send_halos(0)
            send_halos(1)

    for r in range(2):
        wait_bytes(query_win.at[r], q_sem.at[r])
        for side in range(2):
            wait_bytes(win.at[r, :, :, pl.ds(0, HALO), :], halo_sem.at[r, side])

    shifts = [window_off[2 * lat + head] + OFF_MAX for head in range(2)]
    step = jnp.where(iota((SHIFTED, LANES), 1) < 64, shifts[0], shifts[1]) >> 4
    biases = [window_bias(head, shifts[head] & (GROUP - 1)) for head in range(2)]

    @pl.loop(0, LAT)
    def _(s):
        shift_windows(s, step, win, shifted)

    for half in range(2):

        @pl.loop(0, 2)
        def _(block):
            attend_block((2 * half + block) * GROUP, biases, query_win, shifted, attended)

        cols = pl.ds(32 * half, 32)
        send_to_all(
            lambda to: attended.at[to, :, cols, :],
            lambda s: attended_own.at[:, cols, lanes_of(s)],
            att_send.at[half],
            att_sem.at[half],
        )
    loads[8].wait()
    for half in range(2):
        wait_bytes(attended_own.at[:, pl.ds(32 * half, 32), :], att_sem.at[half])
    rows = attended_own[...].reshape(2 * COLS, WIDTH)
    result = tokens[...].reshape(2 * COLS, WIDTH) + dot(rows, proj_w[...])
    updated[...] = result.astype(BF16).reshape(2, COLS, WIDTH)

    wait_bytes(pix_all.at[pl.ds(0, LON - 1)], pix_sem.at[1])
    wait_bytes(pw_all.at[pl.ds(0, LON - 1)], pw_sem.at[1])
    for r in range(2):
        wait_bytes(win.at[r, :, pl.ds(0, LAT - 1), pl.ds(0, COLS), :], kv_send.at[r])
        wait_bytes(query_win.at[r, pl.ds(0, LAT - 1)], q_send.at[r])
        for side in range(2):
            wait_bytes(win.at[r, :, :, pl.ds(0, HALO), :], halo_send.at[r, side])
        wait_bytes(attended.at[pl.ds(0, LAT - 1), :, pl.ds(0, 32), :], att_send.at[r])


def per_device(
    pixels,
    patch_w,
    var_embed,
    var_ids,
    agg_score,
    agg_value,
    agg_out,
    pos_embed,
    norm_gain,
    w_query,
    w_key,
    w_value,
    w_proj,
    window_off,
):
    hbm = pl.BlockSpec(memory_space=pl.ANY)
    vmem = pl.BlockSpec(memory_space=pltpu.VMEM)
    smem = pl.BlockSpec(memory_space=pltpu.SMEM)
    square = pltpu.VMEM((WIDTH, WIDTH), BF16)
    dma = pltpu.SemaphoreType.DMA
    scratch = [
        pltpu.VMEM((VARS, 4, LANES), F32),
        pltpu.VMEM((VARS, 4, WIDTH), BF16),
        pltpu.VMEM((VARS, WIDTH), BF16),
        pltpu.VMEM((WIDTH, HEADS), BF16),
        pltpu.VMEM((HEADS, WIDTH), BF16),
        square,
        square,
        pltpu.VMEM((2, COLS, WIDTH), BF16),
        square,
        square,
        square,
        square,
        pltpu.VMEM((256, 256), BF16),
        pltpu.VMEM((256, 256), BF16),
        pltpu.VMEM((GROUP, 512), F32),
        pltpu.VMEM((VARS, WIDTH), BF16),
        pltpu.VMEM((4 * VARS, WIDTH), F32),
        pltpu.VMEM((2, 256, WIDTH), BF16),
        pltpu.VMEM((4 * VARS, LANES), F32),
        pltpu.VMEM((LANES, 4 * VARS), F32),
        pltpu.VMEM((2, 2, COLS, 256), BF16),
        pltpu.VMEM((512, WIDTH), BF16),
        pltpu.VMEM((HEADS, COLS, WIDTH), BF16),
        pltpu.VMEM((COLS, WIDTH), BF16),
        pltpu.VMEM((2, COLS, WIDTH), F32),
        pltpu.VMEM((COLS, WIDTH), BF16),
        pltpu.VMEM((2, COLS, WIDTH), BF16),
        pltpu.VMEM((2, 2, COLS, WIDTH), BF16),
        pltpu.VMEM((2, LAT, COLS, LANES), BF16),
        pltpu.VMEM((2, 2, LAT, FRAME, LANES), BF16),
        pltpu.VMEM((2, 2, LAT, SHIFTED, LANES), BF16),
        pltpu.VMEM((LAT, 2, COLS, LANES), BF16),
        pltpu.VMEM((2, COLS, WIDTH), BF16),
        dma((9,)),
        dma((2,)),
        dma((2,)),
        dma((2, LAT)),
        dma((2,)),
        dma((2,)),
        dma((2,)),
        dma((2, 2)),
        dma((2, 2)),
        dma((2,)),
        dma((2,)),
    ]
    return pl.pallas_call(
        kernel,
        out_shape=jax.ShapeDtypeStruct((2, COLS, WIDTH), BF16),
        in_specs=[hbm, hbm, hbm, vmem, hbm, hbm, hbm, hbm, vmem, hbm, hbm, hbm, hbm, smem],
        out_specs=vmem,
        scratch_shapes=scratch,
        compiler_params=pltpu.CompilerParams(
            collective_id=0, has_side_effects=True, vmem_limit_bytes=48 * 1024 * 1024
        ),
        name="weather_step",
    )(
        pixels,
        patch_w,
        var_embed,
        var_ids.reshape(1, VARS),
        agg_score,
        agg_value,
        agg_out,
        pos_embed,
        norm_gain.reshape(1, WIDTH),
        w_query,
        w_key,
        w_value,
        w_proj,
        window_off,
    )


def solution(mesh):
    placed = (
        P("lon", "lat", None),
        P("lon", None, None),
        P(),
        P(),
        P(),
        P(),
        P(),
        P("lat", "lon", None),
        P(),
        P(),
        P(),
        P(),
        P(),
        P(),
    )
    return jax.shard_map(
        per_device, mesh=mesh, in_specs=placed, out_specs=P("lat", "lon", None), check_vma=False
    )
```
